32 devices in a mesh: depth: 4 (over x, core), tile: 8 (over z, y).
Axes of the slice: x: 2, y: 2, z: 4, core: 2. Of those that a mesh axis runs over, the one named last changes fastest.
Arguments:
- volume: bfloat16 [256, 128, 1024], P('depth', 'tile'), may hold values from -6 to 6
- knot_pos: int32 [16], replicated, may hold values from 0 to 255, as said below
- knot_color: int32 [4, 16], replicated, may hold values from 0 to 255
Outputs:
- image: float32 [4, 128, 1024], P(None, 'tile', 'depth')
The draws below stay inside these ranges and needn't reach their ends.
Inputs may be any that keep to these rules, and one draw needn't show every extreme that they name: `knot_pos`: strictly increasing with neighbouring breakpoints 9 or more apart; the first is 0 and the last 255.
All inputs are finite; a program needn't handle non-finite values.
Results may differ from the reference program's by a relative error of at most 0.0003.
Values may be sent and summed in bfloat16 or wider, within the bound.
A program may use at most 128 MiB of HBM per device.

```python
import jax
import jax.numpy as jnp
from jax import lax

NY = 1024
KNOTS = 16
CX = 16
NX = 128
NZ = 256
N_TILE = 8


def draw_knot_pos(key, part):
    offsets = jax.random.randint(key, (KNOTS - 2,), -4, 5).astype(jnp.int32)
    inner = (jnp.arange(1, KNOTS - 1, dtype=jnp.int32) * 17 + offsets).astype(jnp.int32)
    first = jnp.zeros((1,), jnp.int32)
    final = jnp.full((1,), 255, jnp.int32)
    return jnp.concatenate([first, inner, final]).astype(jnp.int32)


def touch_ends(entries, stream_key, smallest, top_value):
    place = [jax.random.randint(jax.random.fold_in(stream_key, axis), (), 0, length) for axis, length in enumerate(entries.shape)]
    main_axis = entries.shape.index(max(entries.shape))
    neighbour = place[:main_axis] + [(place[main_axis] + 1) % entries.shape[main_axis]] + place[main_axis + 1:]
    return entries.at[tuple(place)].set(smallest).at[tuple(neighbour)].set(top_value)


def shard_levels(stream_key, extent, pieces, smallest, high):
    factor_of = 1.0
    for position, parts in pieces:
        heights = jax.random.uniform(jax.random.fold_in(jax.random.fold_in(stream_key, 6), position), (parts,), jnp.float32, smallest / len(pieces), high / len(pieces))
        factor_of = factor_of * jnp.repeat(jnp.exp(heights), extent[position] // parts).reshape((-1,) + (1,) * (len(extent) - 1 - position))
    return factor_of


def gaussian(own_key, shape, deviation, reach, shards=(), held_as=jnp.bfloat16):
    gain = shard_levels(own_key, shape, shards, -0.22, 0.18) if shards else 1.0
    result = jax.random.normal(own_key, shape, jnp.float32) * deviation * gain
    return jnp.minimum(jnp.maximum(result, -reach), reach).astype(held_as)


def setup_inputs(seed: int = 0) -> dict:
    streams_of = jax.random.split(jax.random.key(seed), 4)
    return {
        "volume": gaussian(streams_of[0], (NZ, NX, NY), 1.0, 6.0, ((0, 4), (1, 8))),
        "knot_pos": draw_knot_pos(jax.random.fold_in(streams_of[3], 71), 0),
        "knot_color": touch_ends(jax.random.randint(streams_of[2], (4, KNOTS), 0, 256), jax.random.fold_in(streams_of[2], 1), 0, 255).astype(jnp.int32),
    }


def next_along(center):
    return jnp.pad(center[:, :, 1:], ((0, 0), (0, 0), (0, 1)))

def prior_along(center):
    return jnp.pad(center[:, :, :-1], ((0, 0), (0, 0), (1, 0)))

def smooth_block(extended):
    field = extended.astype(jnp.float32)
    center = field[1:-1, 1:-1]
    neighbours = field[2:, 1:-1] + field[:-2, 1:-1] + field[1:-1, 2:] + field[1:-1, :-2]
    neighbours = neighbours + next_along(center) + prior_along(center)
    return 0.4 * center + 0.1 * neighbours

def hat_colors(lookup, knot_pos, knot_color):
    knot_float = knot_pos.astype(jnp.float32)
    palette = knot_color.astype(jnp.float32) / 255.0
    count = knot_pos.shape[0]
    colors = [jnp.zeros_like(lookup) for c in range(3)]
    extinction = jnp.zeros_like(lookup)
    for k in range(count):
        if k == 0:
            weight = jnp.clip((knot_float[1] - lookup) / (knot_float[1] - knot_float[0]), 0.0, 1.0)
        elif k == count - 1:
            weight = jnp.clip((lookup - knot_float[k - 1]) / (knot_float[k] - knot_float[k - 1]), 0.0, 1.0)
        else:
            rising = (lookup - knot_float[k - 1]) / (knot_float[k] - knot_float[k - 1])
            falling = (knot_float[k + 1] - lookup) / (knot_float[k + 1] - knot_float[k])
            weight = jnp.maximum(0.0, jnp.minimum(rising, falling))
        colors = [colors[c] + weight * palette[c, k] for c in range(3)]
        extinction = extinction + weight * palette[3, k]
    return (colors, extinction)

def shade_classify(smooth_ext, knot_pos, knot_color, sigma_scale):
    field = smooth_ext.astype(jnp.float32)
    center = field[1:-1, 1:-1]
    slope_z = 0.5 * (field[2:, 1:-1] - field[:-2, 1:-1])
    slope_x = 0.5 * (field[1:-1, 2:] - field[1:-1, :-2])
    slope_y = 0.5 * (next_along(center) - prior_along(center))
    facing = jnp.abs(0.6 * slope_z + 0.8 * slope_x)
    shading = 0.3 + 0.7 * facing / jnp.sqrt(slope_z * slope_z + slope_x * slope_x + slope_y * slope_y + 0.1)
    knot_float = knot_pos.astype(jnp.float32)
    lookup = jnp.clip(127.5 + 70.0 * center, knot_float[0], knot_float[-1])
    colors, extinction = hat_colors(lookup, knot_pos, knot_color)
    return (shading, colors, extinction * sigma_scale)

def composite(shading, colors, extinction):
    before = jnp.cumsum(extinction, axis=0) - extinction
    weight = shading * (1.0 - jnp.exp(-extinction)) * jnp.exp(-before)
    brick_color = jnp.stack([lax.optimization_barrier(jnp.sum(weight * colors[c], axis=0)) for c in range(3)])
    return (brick_color, lax.optimization_barrier(jnp.sum(extinction, axis=0)))

def reference(volume, knot_pos, knot_color):
    sigma_scale = 4.0 / NZ
    padded = jnp.pad(volume, ((2, 2), (2, 2), (0, 0)))
    z_pos = jnp.arange(NZ + 2, dtype=jnp.int32) - 1
    z_inside = (z_pos >= 0) & (z_pos < NZ)

    def one_block(block):
        start = (block * CX).astype(jnp.int32)
        slab = lax.dynamic_slice_in_dim(padded, start, CX + 4, 1)
        smoothed = smooth_block(slab)
        x_pos = start - 1 + jnp.arange(CX + 2, dtype=jnp.int32)
        x_inside = (x_pos >= 0) & (x_pos < NX)
        inside = z_inside[:, None, None] & x_inside[None, :, None]
        smooth_ext = jnp.where(inside, smoothed, 0.0).astype(jnp.bfloat16)
        shading, colors, extinction = shade_classify(smooth_ext, knot_pos, knot_color, sigma_scale)
        brick_color, optical_depth = composite(shading, colors, extinction)
        return jnp.concatenate([brick_color, (1.0 - jnp.exp(-optical_depth))[None]], axis=0)
    blocks = lax.map(one_block, jnp.arange(N_TILE, dtype=jnp.int32))
    return jnp.transpose(blocks, (1, 0, 2, 3)).reshape(4, NX, NY)
```

```python
import functools
import math

import jax
import jax.numpy as jnp
import numpy as np
from jax import lax
from jax.experimental import pallas as pl
from jax.experimental.pallas import tpu as pltpu
from jax.sharding import PartitionSpec as P

ZB = 16
CB = 256


def windows(width):
    last = width - 2 * CB
    return [min(max(j * CB - CB // 2, 0), last) for j in range(width // CB)]


def along_y(width, before, after):
    mats, index = [], []
    for j, start in enumerate(windows(width)):
        offset = j * CB - start
        if offset not in index:
            index.append(offset)
            k = np.arange(2 * CB)[:, None] - offset
            n = np.arange(CB)[None, :]
            mats.append(before * (k == n - 1) + after * (k == n + 1))
    return np.stack(mats).astype(jnp.bfloat16)


def window_kind(width):
    kinds = []
    out = []
    for j, start in enumerate(windows(width)):
        offset = j * CB - start
        if offset not in kinds:
            kinds.append(offset)
        out.append(kinds.index(offset))
    return out


def constants(planes, rows, width):
    m = ZB * rows
    a = np.zeros((m, m + 2 * rows + 2 * ZB), np.float32)
    dx = np.zeros((m, m + 2 * ZB), np.float32)
    for z in range(ZB):
        for x in range(rows):
            o = z * rows + x
            c = o + rows
            a[o, c] += 4
            a[o, c - rows] += 1
            a[o, c + rows] += 1
            a[o, c - 1 if x else m + 2 * rows + z] += 1
            a[o, c + 1 if x < rows - 1 else m + 2 * rows + ZB + z] += 1
            dx[o, o - 1 if x else m + z] -= 1
            dx[o, o + 1 if x < rows - 1 else m + ZB + z] += 1
    ae = np.zeros((2 * rows, 6 * rows + 4 * ZB), np.float32)
    low_corner = [ZB - 1, 2 * ZB]
    high_corner = [2 * ZB - 1, 3 * ZB]
    for e in range(2):
        for x in range(rows):
            o = e * rows + x
            c = 3 * rows * e + rows + x
            ae[o, c] += 4
            ae[o, c - rows] += 1
            ae[o, c + rows] += 1
            ae[o, c - 1 if x else 6 * rows + low_corner[e]] += 1
            ae[o, c + 1 if x < rows - 1 else 6 * rows + high_corner[e]] += 1
    be = np.zeros((2, planes, 3 * planes + 4 * ZB), np.float32)
    for s, corner in enumerate((low_corner, high_corner)):
        for z in range(planes):
            be[s, z, z] += 4
            be[s, z, z - 1 if z else planes + corner[0]] += 1
            be[s, z, z + 1 if z < planes - 1 else planes + corner[1]] += 1
            be[s, z, planes + 4 * ZB + z] += 1
            be[s, z, 2 * planes + 4 * ZB + z] += 1
    bf = lambda t: t.astype(jnp.bfloat16)
    return [bf(a), bf(dx), bf(ae), bf(be), along_y(width, 1, 1), along_y(width, -1, 1)]


def dot(a, b):
    return jnp.dot(a, b, preferred_element_type=jnp.float32)


def compute(
    table, mask, vol, zlo, zhi, hlo, hhi, inner, corners, a_m, dx_m, ae_m, be_m, sy_m, dy_m,
    out, field, sm, slo, shi, sf, gx, gy,
):
    planes, rows, width = vol.shape
    kind, starts = window_kind(width), windows(width)
    blocks = len(starts)
    m = ZB * rows
    count = table.shape[1]

    field[0 : 2 * rows] = zlo[...].reshape(2 * rows, width)
    field[2 * rows : (planes + 2) * rows] = vol[...].reshape(planes * rows, width)
    field[(planes + 2) * rows :] = zhi[...].reshape(2 * rows, width)

    def cols(j):
        return slice(j * CB, (j + 1) * CB)

    def win(j):
        return slice(starts[j], starts[j] + 2 * CB)

    for j in range(blocks):
        edge_in = jnp.concatenate(
            [field[0 : 3 * rows, cols(j)], field[(planes + 1) * rows :, cols(j)], corners[:, cols(j)]],
            axis=0,
        )
        edge_own = jnp.concatenate(
            [field[rows : 2 * rows, win(j)], field[(planes + 2) * rows : (planes + 3) * rows, win(j)]],
            axis=0,
        )
        edge = 0.1 * (dot(ae_m[...], edge_in) + dot(edge_own, sy_m[kind[j]]))
        low = (edge[:rows] * mask[0]).astype(jnp.bfloat16)
        high = (edge[rows:] * mask[1]).astype(jnp.bfloat16)
        sm[0:rows, cols(j)] = low
        sm[(planes + 1) * rows :, cols(j)] = high
        sf[0:rows, cols(j)] = low.astype(jnp.float32)
        sf[(planes + 1) * rows :, cols(j)] = high.astype(jnp.float32)
        for s, (near, far, dst) in enumerate(
            ((hlo[1], hlo[0], slo), (hhi[0], hhi[1], shi))
        ):
            side_in = jnp.concatenate(
                [near[:, cols(j)], corners[:, cols(j)], far[:, cols(j)], inner[s, :, cols(j)]], axis=0
            )
            side = 0.1 * (dot(be_m[s], side_in) + dot(near[:, win(j)], sy_m[kind[j]]))
            dst[:, cols(j)] = (side * mask[2 + s]).astype(jnp.bfloat16)

    def smooth(zb, carry):
        first = pl.multiple_of((zb * ZB + 1) * rows, rows)
        own = pl.multiple_of((zb * ZB + 2) * rows, rows)
        put = pl.multiple_of((zb * ZB + 1) * rows, rows)
        zs = pl.ds(pl.multiple_of(zb * ZB, ZB), ZB)
        for j in range(blocks):
            near = jnp.concatenate(
                [field[pl.ds(first, m + 2 * rows), cols(j)], hlo[1, zs, cols(j)], hhi[0, zs, cols(j)]],
                axis=0,
            )
            value = dot(a_m[...], near) + dot(field[pl.ds(own, m), win(j)], sy_m[kind[j]])
            rounded = (0.1 * value).astype(jnp.bfloat16)
            sm[pl.ds(put, m), cols(j)] = rounded
            sf[pl.ds(put, m), cols(j)] = rounded.astype(jnp.float32)
        return carry

    lax.fori_loop(0, planes // ZB, smooth, 0)

    def slopes(zb, carry):
        own = pl.multiple_of((zb * ZB + 1) * rows, rows)
        put = pl.multiple_of(zb * ZB * rows, rows)
        zs = pl.ds(pl.multiple_of(zb * ZB, ZB), ZB)
        for j in range(blocks):
            near = jnp.concatenate(
                [sm[pl.ds(own, m), cols(j)], slo[zs, cols(j)], shi[zs, cols(j)]], axis=0
            )
            gx[pl.ds(put, m), cols(j)] = dot(dx_m[...], near)
            gy[pl.ds(put, m), cols(j)] = dot(sm[pl.ds(own, m), win(j)], dy_m[kind[j]])
        return carry

    lax.fori_loop(0, planes // ZB, slopes, 0)

    halves = rows // 8
    step = 4
    knots = [table[0, k] for k in range(count)]
    drops = [table[4, k] for k in range(count)]
    base = table[5, 3]

    def piece(p, carry):
        row = (p % halves) * 8
        col = pl.ds(pl.multiple_of((p // halves) * 128, 128), 128)

        def at(z):
            return pl.ds(pl.multiple_of(z * rows + row, 8), 8)

        def march(i, state):
            prev, here, tau, through, total, line, *bends = state
            for u in range(step):
                z = i * step + u
                after = sf[at(z + 2), col]
                sx, sy = gx[at(z), col], gy[at(z), col]
                sz = after - prev
                facing = jnp.abs(0.42 * sz + 0.56 * sx)
                shading = 0.3 + facing * lax.rsqrt(sz * sz + sx * sx + (sy * sy + 0.4))
                x = jnp.minimum(jnp.maximum(here, knots[0]), knots[count - 1])
                tops = [jnp.maximum(x, knots[k]) for k in range(1, count - 1)]
                terms = [base + drops[0] * x] + [drops[k] * tops[k - 1] for k in range(1, count - 1)]
                while len(terms) > 1:
                    terms = [
                        terms[t] + terms[t + 1] if t + 1 < len(terms) else terms[t]
                        for t in range(0, len(terms), 2)
                    ]
                tau = tau + terms[0]
                left = jnp.exp2(tau)
                weight = shading * (through - left)
                through = left
                total = total + weight
                line = line + weight * x
                bends = [bends[k] + weight * tops[k] for k in range(count - 2)]
                prev, here = here, after
            return (prev, here, tau, through, total, line, *bends)

        zero = jnp.zeros((8, 128), jnp.float32)
        state = (sf[at(0), col], sf[at(1), col], zero, zero + 1.0) + (zero,) * count
        _, _, tau, _, total, line, *bends = lax.fori_loop(0, planes // step, march, state)
        for c in range(3):
            value = table[5, c] * total + table[1 + c, 0] * line
            for k in range(1, count - 1):
                value = value + table[1 + c, k] * bends[k - 1]
            out[c, pl.ds(row, 8), col] = value
        out[3, pl.ds(row, 8), col] = tau
        return carry

    lax.fori_loop(0, halves * (width // 128), piece, 0)


def transfer_table(knot_pos, knot_color, depth_cells):
    at = (knot_pos.astype(jnp.float32) - 127.5) / 70.0
    scale = jnp.array([1 / 255.0] * 3 + [-4.0 * math.log2(math.e) / depth_cells / 255.0], jnp.float32)
    value = knot_color.astype(jnp.float32) * scale[:, None]
    slope = (value[:, 1:] - value[:, :-1]) / (at[1:] - at[:-1])
    bend = jnp.concatenate([slope[:, :1], slope[:, 1:] - slope[:, :-1]], axis=1)
    bend = jnp.pad(bend, ((0, 0), (0, 1)))
    const = value[:, 0] - jnp.sum(bend * at[None], axis=1)
    const = jnp.pad(const, (0, at.shape[0] - 4))
    return jnp.concatenate([at[None], bend, const[None]], axis=0)


def shift(value, axes, sizes, steps):
    pairs = []
    for i in range(sizes[0]):
        for j in range(sizes[1]):
            k, l = i + steps[0], j + steps[1]
            if 0 <= k < sizes[0] and 0 <= l < sizes[1]:
                pairs.append((i * sizes[1] + j, k * sizes[1] + l))
    return lax.ppermute(value, axes, pairs)


def solution(mesh):
    axes = ("depth", "tile")
    sizes = tuple(mesh.shape[a] for a in axes)

    def body(volume, knot_pos, knot_color):
        planes, rows, width = volume.shape
        go = functools.partial(shift, axes=axes, sizes=sizes)
        zlo = go(volume[planes - 2 :], steps=(1, 0))
        zhi = go(volume[:2], steps=(-1, 0))
        first = jnp.transpose(volume[:, :2], (1, 0, 2))
        last = jnp.transpose(volume[:, rows - 2 :], (1, 0, 2))
        hlo = go(last, steps=(0, 1))
        hhi = go(first, steps=(0, -1))
        inner = jnp.stack([first[0], last[1]])
        corners = jnp.concatenate(
            [
                go(last[1, planes - ZB :], steps=(1, 1)),
                go(first[0, planes - ZB :], steps=(1, -1)),
                go(last[1, :ZB], steps=(-1, 1)),
                go(first[0, :ZB], steps=(-1, -1)),
            ],
            axis=0,
        )
        d, t = lax.axis_index("depth"), lax.axis_index("tile")
        mask = jnp.stack([d > 0, d < sizes[0] - 1, t > 0, t < sizes[1] - 1]).astype(jnp.float32)
        table = transfer_table(knot_pos, knot_color, planes * sizes[0])
        consts = [jnp.asarray(c) for c in constants(planes, rows, width)]
        smem = pl.BlockSpec(memory_space=pltpu.SMEM)
        vmem = pl.BlockSpec(memory_space=pltpu.VMEM)
        brick = pl.pallas_call(
            compute,
            out_shape=jax.ShapeDtypeStruct((4, rows, width), jnp.float32),
            in_specs=[smem, smem] + [vmem] * (7 + len(consts)),
            out_specs=vmem,
            scratch_shapes=[
                pltpu.VMEM(((planes + 4) * rows, width), jnp.bfloat16),
                pltpu.VMEM(((planes + 2) * rows, width), jnp.bfloat16),
                pltpu.VMEM((planes, width), jnp.bfloat16),
                pltpu.VMEM((planes, width), jnp.bfloat16),
                pltpu.VMEM(((planes + 2) * rows, width), jnp.float32),
                pltpu.VMEM((planes * rows, width), jnp.float32),
                pltpu.VMEM((planes * rows, width), jnp.float32),
            ],
            compiler_params=pltpu.CompilerParams(vmem_limit_bytes=48 << 20),
        )(table, mask, volume, zlo, zhi, hlo, hhi, inner, corners, *consts)
        part = width // sizes[0]
        split = brick.reshape(4, rows, sizes[0], part)
        parts = lax.all_to_all(split, "depth", split_axis=2, concat_axis=0, tiled=False)
        colors = jnp.zeros((3, rows, part), jnp.float32)
        ahead = jnp.zeros((rows, part), jnp.float32)
        for i in range(sizes[0]):
            colors = colors + parts[i, :3] * jnp.exp2(ahead)[None]
            ahead = ahead + parts[i, 3]
        return jnp.concatenate([colors, (1.0 - jnp.exp2(ahead))[None]], axis=0)

    in_specs = (P("depth", "tile", None), P(), P())
    return jax.shard_map(
        body, mesh=mesh, in_specs=in_specs, out_specs=P(None, "tile", "depth"), check_vma=False
    )
```

```python
import functools
import math

import jax
import jax.numpy as jnp
import numpy as np
from jax import lax
from jax.experimental import pallas as pl
from jax.experimental.pallas import tpu as pltpu
from jax.sharding import PartitionSpec as P

ZB = 16
CB = 256


def windows(width):
    last = width - 2 * CB
    return [min(max(j * CB - CB // 2, 0), last) for j in range(width // CB)]


def along_y(width, before, after):
    mats, index = [], []
    for j, start in enumerate(windows(width)):
        offset = j * CB - start
        if offset not in index:
            index.append(offset)
            k = np.arange(2 * CB)[:, None] - offset
            n = np.arange(CB)[None, :]
            mats.append(before * (k == n - 1) + after * (k == n + 1))
    return np.stack(mats).astype(jnp.bfloat16)


def window_kind(width):
    kinds = []
    out = []
    for j, start in enumerate(windows(width)):
        offset = j * CB - start
        if offset not in kinds:
            kinds.append(offset)
        out.append(kinds.index(offset))
    return out


def constants(planes, rows, width):
    m = ZB * rows
    a = np.zeros((m, m + 2 * rows + 2 * ZB), np.float32)
    dx = np.zeros((m, m + 2 * ZB), np.float32)
    for z in range(ZB):
        for x in range(rows):
            o = z * rows + x
            c = o + rows
            a[o, c] += 4
            a[o, c - rows] += 1
            a[o, c + rows] += 1
            a[o, c - 1 if x else m + 2 * rows + z] += 1
            a[o, c + 1 if x < rows - 1 else m + 2 * rows + ZB + z] += 1
            dx[o, o - 1 if x else m + z] -= 1
            dx[o, o + 1 if x < rows - 1 else m + ZB + z] += 1
    ae = np.zeros((2 * rows, 6 * rows + 4 * ZB), np.float32)
    low_corner = [ZB - 1, 2 * ZB]
    high_corner = [2 * ZB - 1, 3 * ZB]
    for e in range(2):
        for x in range(rows):
            o = e * rows + x
            c = 3 * rows * e + rows + x
            ae[o, c] += 4
            ae[o, c - rows] += 1
            ae[o, c + rows] += 1
            ae[o, c - 1 if x else 6 * rows + low_corner[e]] += 1
            ae[o, c + 1 if x < rows - 1 else 6 * rows + high_corner[e]] += 1
    be = np.zeros((2, planes, 3 * planes + 4 * ZB), np.float32)
    for s, corner in enumerate((low_corner, high_corner)):
        for z in range(planes):
            be[s, z, z] += 4
            be[s, z, z - 1 if z else planes + corner[0]] += 1
            be[s, z, z + 1 if z < planes - 1 else planes + corner[1]] += 1
            be[s, z, planes + 4 * ZB + z] += 1
            be[s, z, 2 * planes + 4 * ZB + z] += 1
    pack = np.zeros((4 * ZB, m), np.float32)
    for r, row in enumerate((0, 1, rows - 2, rows - 1)):
        for z in range(ZB):
            pack[r * ZB + z, z * rows + row] = 1
    bf = lambda t: t.astype(jnp.bfloat16)
    return [bf(pack), along_y(width, 1, 1), bf(a), bf(ae), bf(be), bf(dx), along_y(width, -1, 1)]


def dot(a, b):
    return jnp.dot(a, b, preferred_element_type=jnp.float32)


def compute(
    sizes, knot_pos, knot_color, vol,
    pack_h, sy_h, a_h, ae_h, be_h, dx_h, dy_h,
    out, field, packed, hlo, hhi, corners, sm, slo, shi, sf, gx, gy, tab, stage, parts,
    pack_m, sy_m, a_m, ae_m, be_m, dx_m, dy_m,
    vol_sem, const_sem, z_send, z_recv, x_send, x_recv, c_send, c_recv, f_send, f_recv,
):
    rows, width = out.shape[1], vol.shape[1]
    planes = vol.shape[0] // rows
    depths, tiles = sizes
    d, t = lax.axis_index("depth"), lax.axis_index("tile")
    kind, starts = window_kind(width), windows(width)
    blocks = len(starts)
    groups = planes // ZB
    m = ZB * rows
    count = knot_pos.shape[0]

    loads = []
    for zb in range(groups):
        loads.append(
            pltpu.make_async_copy(
                vol.at[pl.ds(zb * m, m)],
                field.at[pl.ds(2 * rows + zb * m, m)],
                vol_sem.at[zb],
            )
        )
    fetches = [
        pltpu.make_async_copy(src, dst, const_sem.at[i])
        for i, (src, dst) in enumerate(
            (
                (pack_h, pack_m), (sy_h, sy_m), (a_h, a_m), (ae_h, ae_m),
                (be_h, be_m), (dx_h, dx_m), (dy_h, dy_m),
            )
        )
    ]
    fetches[0].start()
    for copy in loads + fetches[1:]:
        copy.start()

    barrier = pltpu.get_barrier_semaphore()

    def hello(depth, tile):
        pl.semaphore_signal(
            barrier, inc=1, device_id=(depth, tile), device_id_type=pl.DeviceIdType.MESH
        )

    lower, upper = t > 0, t < tiles - 1
    nearer, farther = d > 0, d < depths - 1
    near_d, far_d = jnp.maximum(d - 1, 0), jnp.minimum(d + 1, depths - 1)
    low_t, up_t = jnp.maximum(t - 1, 0), jnp.minimum(t + 1, tiles - 1)
    for k in range(1, depths):
        hello(lax.rem(d + k, depths), t)
    for there, tile in ((lower, low_t), (upper, up_t)):
        pl.when(there)(functools.partial(hello, d, tile))
        pl.when(there & nearer)(functools.partial(hello, near_d, tile))
        pl.when(there & farther)(functools.partial(hello, far_d, tile))
    number = lambda flag: jnp.where(flag, 1, 0)
    greeted = (depths - 1) + (number(lower) + number(upper)) * (
        1 + number(nearer) + number(farther)
    )

    def splat(value):
        return jnp.full((8, 128), value, jnp.int32).astype(jnp.float32)

    at = [(splat(knot_pos[k]) - 127.5) * (1.0 / 70.0) for k in range(count)]
    gaps = [1.0 / (at[k + 1] - at[k]) for k in range(count - 1)]
    for k in range(count):
        tab[k] = at[k]
    scales = [1 / 255.0] * 3 + [-4.0 * math.log2(math.e) / (planes * depths) / 255.0]
    for c in range(4):
        value = [splat(knot_color[c, k]) * scales[c] for k in range(count)]
        const, before = value[0], None
        for k in range(count - 1):
            slope = (value[k + 1] - value[k]) * gaps[k]
            bend = slope if k == 0 else slope - before
            before = slope
            const = const - bend * at[k]
            tab[count * (c + 1) + k] = bend
        tab[count * (c + 1) + count - 1] = const

    def cols(j):
        return slice(j * CB, (j + 1) * CB)

    def win(j):
        return slice(starts[j], starts[j] + 2 * CB)

    fetches[0].wait()
    for zb in range(groups):
        loads[zb].wait()
        for j in range(blocks):
            picked = dot(pack_m[...], field[2 * rows + zb * m : 2 * rows + (zb + 1) * m, cols(j)])
            picked = picked.astype(jnp.bfloat16)
            for r in range(4):
                packed[r, zb * ZB : (zb + 1) * ZB, cols(j)] = picked[r * ZB : (r + 1) * ZB]

    pl.semaphore_wait(barrier, greeted)

    def remote(src, dst, send, recv, depth, tile):
        return pltpu.make_async_remote_copy(
            src_ref=src, dst_ref=dst, send_sem=send, recv_sem=recv,
            device_id=(depth, tile), device_id_type=pl.DeviceIdType.MESH,
        )

    inside, end = 2 * rows, (planes + 2) * rows
    z_copies, x_copies, c_copies = [], [], []
    for i, (src, dst, depth, sends, receives) in enumerate(
        (
            (end - 2 * rows, 0, far_d, farther, nearer),
            (inside, end, near_d, nearer, farther),
        )
    ):
        target = field.at[pl.ds(dst, 2 * rows)]
        z_copies.append(
            (
                remote(
                    field.at[pl.ds(src, 2 * rows)], target,
                    z_send.at[i], z_recv.at[i], depth, t,
                ),
                sends, receives, target,
            )
        )
    for zb in range(groups):
        zs = pl.ds(zb * ZB, ZB)
        for i, (src, halo, tile, sends, receives) in enumerate(
            ((2, hlo, up_t, upper, lower), (0, hhi, low_t, lower, upper))
        ):
            target = halo.at[:, zs]
            n = 2 * zb + i
            x_copies.append(
                (
                    remote(
                        packed.at[pl.ds(src, 2), zs], target,
                        x_send.at[n], x_recv.at[n], d, tile,
                    ),
                    sends, receives, target,
                )
            )
    for i, (row, z, depth, tile, sends, receives) in enumerate(
        (
            (3, planes - ZB, far_d, up_t, farther & upper, nearer & lower),
            (0, planes - ZB, far_d, low_t, farther & lower, nearer & upper),
            (3, 0, near_d, up_t, nearer & upper, farther & lower),
            (0, 0, near_d, low_t, nearer & lower, farther & upper),
        )
    ):
        target = corners.at[pl.ds(i * ZB, ZB)]
        c_copies.append(
            (
                remote(
                    packed.at[row, pl.ds(z, ZB)], target,
                    c_send.at[i], c_recv.at[i], depth, tile,
                ),
                sends, receives, target,
            )
        )
    for copy, sends, receives, target in z_copies + x_copies + c_copies:
        pl.when(sends)(copy.start)

    for copy, sends, receives, target in z_copies + x_copies + c_copies:

        @pl.when(jnp.logical_not(receives))
        def _():
            target[...] = jnp.zeros(target.shape, jnp.bfloat16)

    def arrived(copies):
        for copy, sends, receives, target in copies:
            pl.when(receives)(copy.wait_recv)

    for copy in fetches[1:]:
        copy.wait()

    def smooth(zb):
        first, own = (zb * ZB + 1) * rows, (zb * ZB + 2) * rows
        zs = slice(zb * ZB, (zb + 1) * ZB)
        for j in range(blocks):
            near = jnp.concatenate(
                [field[first : first + m + 2 * rows, cols(j)], hlo[1, zs, cols(j)], hhi[0, zs, cols(j)]],
                axis=0,
            )
            value = dot(a_m[...], near) + dot(field[own : own + m, win(j)], sy_m[kind[j]])
            rounded = (0.1 * value).astype(jnp.bfloat16)
            sm[first : first + m, cols(j)] = rounded
            sf[first : first + m, cols(j)] = rounded.astype(jnp.float32)

    for zb in range(groups):
        if zb == 0:
            arrived(z_copies)
        arrived(x_copies[2 * zb : 2 * zb + 2])
        smooth(zb)
    arrived(c_copies)

    one = lambda flag: jnp.where(flag, 1.0, 0.0)
    for j in range(blocks):
        edge_in = jnp.concatenate(
            [field[0 : 3 * rows, cols(j)], field[(planes + 1) * rows :, cols(j)], corners[:, cols(j)]],
            axis=0,
        )
        edge_own = jnp.concatenate(
            [field[rows : 2 * rows, win(j)], field[(planes + 2) * rows : (planes + 3) * rows, win(j)]],
            axis=0,
        )
        edge = 0.1 * (dot(ae_m[...], edge_in) + dot(edge_own, sy_m[kind[j]]))
        sf[0:rows, cols(j)] = (edge[:rows] * one(nearer)).astype(jnp.bfloat16).astype(jnp.float32)
        sf[(planes + 1) * rows :, cols(j)] = (
            (edge[rows:] * one(farther)).astype(jnp.bfloat16).astype(jnp.float32)
        )
        for s, (halo, near, far, own, dst, there) in enumerate(
            ((hlo, 1, 0, 0, slo, lower), (hhi, 0, 1, 3, shi, upper))
        ):
            side_in = jnp.concatenate(
                [halo[near, :, cols(j)], corners[:, cols(j)], halo[far, :, cols(j)], packed[own, :, cols(j)]],
                axis=0,
            )
            side = 0.1 * (dot(be_m[s], side_in) + dot(halo[near, :, win(j)], sy_m[kind[j]]))
            dst[:, cols(j)] = (side * one(there)).astype(jnp.bfloat16)

    def slopes(zb, carry):
        own = pl.multiple_of((zb * ZB + 1) * rows, rows)
        put = pl.multiple_of(zb * ZB * rows, rows)
        zs = pl.ds(pl.multiple_of(zb * ZB, ZB), ZB)
        for j in range(blocks):
            near = jnp.concatenate(
                [sm[pl.ds(own, m), cols(j)], slo[zs, cols(j)], shi[zs, cols(j)]], axis=0
            )
            gx[pl.ds(put, m), cols(j)] = dot(dx_m[...], near)
            gy[pl.ds(put, m), cols(j)] = dot(sm[pl.ds(own, m), win(j)], dy_m[kind[j]])
        return carry

    lax.fori_loop(0, groups, slopes, 0)

    part = width // depths
    halves = rows // 8
    lanes = part // 128
    step = 4

    def owner(i, carry):
        whose = lax.rem(d + 1 + i, depths)

        def piece(p, carry):
            row = pl.multiple_of(lax.rem(p, halves) * 8, 8)
            place = pl.multiple_of((p // halves) * 128, 128)
            col = pl.ds(pl.multiple_of(whose * part + place, 128), 128)

            def spot(z):
                return pl.ds(pl.multiple_of(z * rows + row, 8), 8)

            def march(i, state):
                prev, here, tau, through, total, line, *bends = state
                for u in range(step):
                    z = i * step + u
                    after = sf[spot(z + 2), col]
                    sx, sy = gx[spot(z), col], gy[spot(z), col]
                    sz = after - prev
                    facing = jnp.abs(0.42 * sz + 0.56 * sx)
                    shading = 0.3 + facing * lax.rsqrt(sz * sz + sx * sx + (sy * sy + 0.4))
                    x = jnp.minimum(jnp.maximum(here, tab[0]), tab[count - 1])
                    tops = [jnp.maximum(x, tab[k]) for k in range(1, count - 1)]
                    terms = [tab[5 * count - 1] + tab[4 * count] * x]
                    terms += [tab[4 * count + k] * tops[k - 1] for k in range(1, count - 1)]
                    while len(terms) > 1:
                        terms = [
                            terms[q] + terms[q + 1] if q + 1 < len(terms) else terms[q]
                            for q in range(0, len(terms), 2)
                        ]
                    tau = tau + terms[0]
                    left = jnp.exp2(tau)
                    weight = shading * (through - left)
                    through = left
                    total = total + weight
                    line = line + weight * x
                    bends = [bends[k] + weight * tops[k] for k in range(count - 2)]
                    prev, here = here, after
                return (prev, here, tau, through, total, line, *bends)

            zero = jnp.zeros((8, 128), jnp.float32)
            state = (sf[spot(0), col], sf[spot(1), col], zero, zero + 1.0) + (zero,) * count
            _, _, tau, _, total, line, *bends = lax.fori_loop(0, planes // step, march, state)
            for c in range(3):
                value = tab[count * (c + 2) - 1] * total + tab[count * (c + 1)] * line
                for k in range(1, count - 1):
                    value = value + tab[count * (c + 1) + k] * bends[k - 1]
                stage[whose, c, pl.ds(row, 8), pl.ds(place, 128)] = value
            stage[whose, 3, pl.ds(row, 8), pl.ds(place, 128)] = tau
            return carry

        lax.fori_loop(0, halves * lanes, piece, 0)

        @pl.when(i < depths - 1)
        def _():
            remote(stage.at[whose], parts.at[d], f_send.at[i], f_recv.at[i], whose, t).start()

        return carry

    lax.fori_loop(0, depths, owner, 0)
    parts[d] = stage[d]
    for i in range(depths - 1):
        whose = lax.rem(d + 1 + i, depths)
        source = lax.rem(d - 1 - i + depths, depths)
        remote(stage.at[whose], parts.at[source], f_send.at[i], f_recv.at[i], whose, t).wait_recv()

    for row in range(0, rows, 8):
        for place in range(0, part, 128):
            spots = (slice(row, row + 8), slice(place, place + 128))
            ahead = parts[(0, 3) + spots]
            colors = [parts[(0, c) + spots] for c in range(3)]
            for i in range(1, depths):
                left = jnp.exp2(ahead)
                colors = [colors[c] + left * parts[(i, c) + spots] for c in range(3)]
                ahead = ahead + parts[(i, 3) + spots]
            for c in range(3):
                out[(c,) + spots] = colors[c]
            out[(3,) + spots] = 1.0 - jnp.exp2(ahead)

    for copy, sends, receives, target in z_copies + x_copies + c_copies:
        pl.when(sends)(copy.wait_send)
    for i in range(depths - 1):
        whose = lax.rem(d + 1 + i, depths)
        remote(stage.at[whose], parts.at[d], f_send.at[i], f_recv.at[i], whose, t).wait_send()


def solution(mesh):
    sizes = (mesh.shape["depth"], mesh.shape["tile"])

    def body(volume, knot_pos, knot_color):
        planes, rows, width = volume.shape
        consts = [jnp.asarray(c) for c in constants(planes, rows, width)]
        part = width // sizes[0]
        bf, f32 = jnp.bfloat16, jnp.float32
        dma = pltpu.SemaphoreType.DMA
        smem = pl.BlockSpec(memory_space=pltpu.SMEM)
        anywhere = pl.BlockSpec(memory_space=pl.ANY)
        return pl.pallas_call(
            functools.partial(compute, sizes),
            out_shape=jax.ShapeDtypeStruct((4, rows, part), f32),
            in_specs=[smem, smem] + [anywhere] * (1 + len(consts)),
            out_specs=pl.BlockSpec(memory_space=pltpu.VMEM),
            scratch_shapes=[
                pltpu.VMEM(((planes + 4) * rows, width), bf),
                pltpu.VMEM((4, planes, width), bf),
                pltpu.VMEM((2, planes, width), bf),
                pltpu.VMEM((2, planes, width), bf),
                pltpu.VMEM((4 * ZB, width), bf),
                pltpu.VMEM(((planes + 2) * rows, width), bf),
                pltpu.VMEM((planes, width), bf),
                pltpu.VMEM((planes, width), bf),
                pltpu.VMEM(((planes + 2) * rows, width), f32),
                pltpu.VMEM((planes * rows, width), f32),
                pltpu.VMEM((planes * rows, width), f32),
                pltpu.VMEM((5 * knot_pos.shape[0], 8, 128), f32),
                pltpu.VMEM((sizes[0], 4, rows, part), f32),
                pltpu.VMEM((sizes[0], 4, rows, part), f32),
            ]
            + [pltpu.VMEM(c.shape, c.dtype) for c in consts]
            + [
                dma((planes // ZB,)), dma((len(consts),)),
                dma((2,)), dma((2,)),
                dma((2 * planes // ZB,)), dma((2 * planes // ZB,)),
                dma((4,)), dma((4,)),
                dma((sizes[0] - 1,)), dma((sizes[0] - 1,)),
            ],
            compiler_params=pltpu.CompilerParams(
                vmem_limit_bytes=48 << 20, collective_id=0, has_side_effects=True
            ),
        )(knot_pos, knot_color, volume.reshape(planes * rows, width), *consts)

    in_specs = (P("depth", "tile", None), P(), P())
    return jax.shard_map(
        body, mesh=mesh, in_specs=in_specs, out_specs=P(None, "tile", "depth"), check_vma=False
    )
```

```python
import functools
import math

import jax
import jax.numpy as jnp
import numpy as np
from jax import lax
from jax.experimental import pallas as pl
from jax.experimental.pallas import tpu as pltpu
from jax.sharding import PartitionSpec as P

ZB = 16
CB = 256


def windows(width):
    last = width - 2 * CB
    return [min(max(j * CB - CB // 2, 0), last) for j in range(width // CB)]


def along_y(width, before, after):
    mats, index = [], []
    for j, start in enumerate(windows(width)):
        offset = j * CB - start
        if offset not in index:
            index.append(offset)
            k = np.arange(2 * CB)[:, None] - offset
            n = np.arange(CB)[None, :]
            mats.append(before * (k == n - 1) + after * (k == n + 1))
    return np.stack(mats).astype(jnp.bfloat16)


def window_kind(width):
    kinds = []
    out = []
    for j, start in enumerate(windows(width)):
        offset = j * CB - start
        if offset not in kinds:
            kinds.append(offset)
        out.append(kinds.index(offset))
    return out


def constants(planes, rows, width):
    m = ZB * rows
    a = np.zeros((m, m + 2 * rows + 2 * ZB), np.float32)
    dx = np.zeros((m, m + 2 * ZB), np.float32)
    for z in range(ZB):
        for x in range(rows):
            o = z * rows + x
            c = o + rows
            a[o, c] += 4
            a[o, c - rows] += 1
            a[o, c + rows] += 1
            a[o, c - 1 if x else m + 2 * rows + z] += 1
            a[o, c + 1 if x < rows - 1 else m + 2 * rows + ZB + z] += 1
            dx[o, o - 1 if x else m + z] -= 1
            dx[o, o + 1 if x < rows - 1 else m + ZB + z] += 1
    ae = np.zeros((2, rows, 3 * rows + 2 * ZB), np.float32)
    for e in range(2):
        beside = 0 if e else ZB - 1
        for x in range(rows):
            c = rows + x
            ae[e, x, c] += 4
            ae[e, x, c - rows] += 1
            ae[e, x, c + rows] += 1
            ae[e, x, c - 1 if x else 3 * rows + beside] += 1
            ae[e, x, c + 1 if x < rows - 1 else 3 * rows + ZB + beside] += 1
    be = np.zeros((ZB, 5 * ZB), np.float32)
    for z in range(ZB):
        be[z, ZB + z] += 4
        be[z, ZB + z - 1] += 1
        be[z, ZB + z + 1] += 1
        be[z, 3 * ZB + z] += 1
        be[z, 4 * ZB + z] += 1
    pack = np.zeros((4 * ZB, m), np.float32)
    for r, row in enumerate((0, 1, rows - 2, rows - 1)):
        for z in range(ZB):
            pack[r * ZB + z, z * rows + row] = 1
    bf = lambda t: t.astype(jnp.bfloat16)
    return [bf(pack), along_y(width, 1, 1), bf(a), bf(ae), bf(be), bf(dx), along_y(width, -1, 1)]


def dot(a, b):
    return jnp.dot(a, b, preferred_element_type=jnp.float32)


def compute(
    sizes, knot_pos, knot_color, vol,
    pack_h, sy_h, a_h, ae_h, be_h, dx_h, dy_h,
    out, field, packed, hlo, hhi, corners, sm, slo, shi, sf, gx, gy, tab, stage, parts, sums,
    pack_m, sy_m, a_m, ae_m, be_m, dx_m, dy_m,
    vol_sem, const_sem, z_send, z_recv, x_send, x_recv, c_send, c_recv, f_send, f_recv,
):
    rows, width = out.shape[1], vol.shape[1]
    planes = vol.shape[0] // rows
    depths, tiles = sizes
    d, t = lax.axis_index("depth"), lax.axis_index("tile")
    kind, starts = window_kind(width), windows(width)
    blocks = len(starts)
    groups = planes // ZB
    m = ZB * rows
    count = knot_pos.shape[0]

    loads = []
    for zb in range(groups):
        loads.append(
            pltpu.make_async_copy(
                vol.at[pl.ds(zb * m, m)],
                field.at[pl.ds(2 * rows + zb * m, m)],
                vol_sem.at[zb],
            )
        )
    fetches = [
        pltpu.make_async_copy(src, dst, const_sem.at[i])
        for i, (src, dst) in enumerate(
            (
                (pack_h, pack_m), (sy_h, sy_m), (a_h, a_m), (ae_h, ae_m),
                (be_h, be_m), (dx_h, dx_m), (dy_h, dy_m),
            )
        )
    ]
    fetches[0].start()
    for copy in loads + fetches[1:]:
        copy.start()

    barrier = pltpu.get_barrier_semaphore()

    def hello(depth, tile):
        pl.semaphore_signal(
            barrier, inc=1, device_id=(depth, tile), device_id_type=pl.DeviceIdType.MESH
        )

    lower, upper = t > 0, t < tiles - 1
    nearer, farther = d > 0, d < depths - 1
    near_d, far_d = jnp.maximum(d - 1, 0), jnp.minimum(d + 1, depths - 1)
    low_t, up_t = jnp.maximum(t - 1, 0), jnp.minimum(t + 1, tiles - 1)
    for k in range(1, depths):
        hello(lax.rem(d + k, depths), t)
    for there, tile in ((lower, low_t), (upper, up_t)):
        pl.when(there)(functools.partial(hello, d, tile))
        pl.when(there & nearer)(functools.partial(hello, near_d, tile))
        pl.when(there & farther)(functools.partial(hello, far_d, tile))
    number = lambda flag: jnp.where(flag, 1, 0)
    greeted = (depths - 1) + (number(lower) + number(upper)) * (
        1 + number(nearer) + number(farther)
    )

    def splat(value):
        return jnp.full((8, 128), value, jnp.int32).astype(jnp.float32)

    at = [(splat(knot_pos[k]) - 127.5) * (1.0 / 70.0) for k in range(count)]
    gaps = [1.0 / (at[k + 1] - at[k]) for k in range(count - 1)]
    for k in range(count):
        tab[k] = at[k]
    scales = [1 / 255.0] * 3 + [-4.0 * math.log2(math.e) / (planes * depths) / 255.0]
    for c in range(4):
        value = [splat(knot_color[c, k]) * scales[c] for k in range(count)]
        const, before = value[0], None
        for k in range(count - 1):
            slope = (value[k + 1] - value[k]) * gaps[k]
            bend = slope if k == 0 else slope - before
            before = slope
            const = const - bend * at[k]
            tab[count * (c + 1) + k] = bend
        tab[count * (c + 1) + count - 1] = const

    def cols(j):
        return slice(j * CB, (j + 1) * CB)

    def win(j):
        return slice(starts[j], starts[j] + 2 * CB)

    fetches[0].wait()
    for zb in range(groups):
        loads[zb].wait()
        for j in range(blocks):
            picked = dot(pack_m[...], field[2 * rows + zb * m : 2 * rows + (zb + 1) * m, cols(j)])
            picked = picked.astype(jnp.bfloat16)
            for r in range(4):
                packed[r, zb * ZB : (zb + 1) * ZB, cols(j)] = picked[r * ZB : (r + 1) * ZB]

    pl.semaphore_wait(barrier, greeted)

    def remote(src, dst, send, recv, depth, tile):
        return pltpu.make_async_remote_copy(
            src_ref=src, dst_ref=dst, send_sem=send, recv_sem=recv,
            device_id=(depth, tile), device_id_type=pl.DeviceIdType.MESH,
        )

    inside, end = 2 * rows, (planes + 2) * rows
    z_copies, x_copies, c_copies = [], [], []
    for i, (src, dst, depth, sends, receives) in enumerate(
        (
            (end - 2 * rows, 0, far_d, farther, nearer),
            (inside, end, near_d, nearer, farther),
        )
    ):
        target = field.at[pl.ds(dst, 2 * rows)]
        z_copies.append(
            (
                remote(
                    field.at[pl.ds(src, 2 * rows)], target,
                    z_send.at[i], z_recv.at[i], depth, t,
                ),
                sends, receives, target,
            )
        )
    for zb in range(groups):
        zs = pl.ds(zb * ZB, ZB)
        for i, (src, halo, tile, sends, receives) in enumerate(
            ((2, hlo, up_t, upper, lower), (0, hhi, low_t, lower, upper))
        ):
            target = halo.at[:, zs]
            n = 2 * zb + i
            x_copies.append(
                (
                    remote(
                        packed.at[pl.ds(src, 2), zs], target,
                        x_send.at[n], x_recv.at[n], d, tile,
                    ),
                    sends, receives, target,
                )
            )
    for i, (row, z, depth, tile, sends, receives) in enumerate(
        (
            (3, planes - ZB, far_d, up_t, farther & upper, nearer & lower),
            (0, planes - ZB, far_d, low_t, farther & lower, nearer & upper),
            (3, 0, near_d, up_t, nearer & upper, farther & lower),
            (0, 0, near_d, low_t, nearer & lower, farther & upper),
        )
    ):
        target = corners.at[pl.ds(i * ZB, ZB)]
        c_copies.append(
            (
                remote(
                    packed.at[row, pl.ds(z, ZB)], target,
                    c_send.at[i], c_recv.at[i], depth, tile,
                ),
                sends, receives, target,
            )
        )
    for copy, sends, receives, target in z_copies + x_copies[:2] + c_copies + x_copies[2:]:
        pl.when(sends)(copy.start)

    for copy, sends, receives, target in z_copies + x_copies + c_copies:

        @pl.when(jnp.logical_not(receives))
        def _():
            target[...] = jnp.zeros(target.shape, jnp.bfloat16)

    def arrived(copies):
        for copy, sends, receives, target in copies:
            pl.when(receives)(copy.wait_recv)

    for copy in fetches[1:]:
        copy.wait()

    def smooth(zb):
        first, own = (zb * ZB + 1) * rows, (zb * ZB + 2) * rows
        zs = slice(zb * ZB, (zb + 1) * ZB)
        for j in range(blocks):
            near = jnp.concatenate(
                [field[first : first + m + 2 * rows, cols(j)], hlo[1, zs, cols(j)], hhi[0, zs, cols(j)]],
                axis=0,
            )
            value = dot(a_m[...], near) + dot(field[own : own + m, win(j)], sy_m[kind[j]])
            rounded = (0.1 * value).astype(jnp.bfloat16)
            sm[first : first + m, cols(j)] = rounded
            sf[first : first + m, cols(j)] = rounded.astype(jnp.float32)

    one = lambda flag: jnp.where(flag, 1.0, 0.0)

    def edge(first, put, corner, there):
        for j in range(blocks):
            near = jnp.concatenate(
                [field[first : first + 3 * rows, cols(j)], corners[corner : corner + 2 * ZB, cols(j)]],
                axis=0,
            )
            own = field[first + rows : first + 2 * rows, win(j)]
            value = 0.1 * (dot(ae_m[corner // (2 * ZB)], near) + dot(own, sy_m[kind[j]]))
            value = (value * one(there)).astype(jnp.bfloat16)
            sf[put : put + rows, cols(j)] = value.astype(jnp.float32)

    def sides(zb):
        zs = slice(zb * ZB, (zb + 1) * ZB)
        for j in range(blocks):
            for s, (halo, near, far, own, dst, there) in enumerate(
                ((hlo, 1, 0, 0, slo, lower), (hhi, 0, 1, 3, shi, upper))
            ):

                def block(b):
                    if b < 0:
                        return corners[s * ZB : (s + 1) * ZB, cols(j)]
                    if b == groups:
                        return corners[(2 + s) * ZB : (3 + s) * ZB, cols(j)]
                    return halo[near, b * ZB : (b + 1) * ZB, cols(j)]

                side_in = jnp.concatenate(
                    [block(zb - 1), block(zb), block(zb + 1), halo[far, zs, cols(j)], packed[own, zs, cols(j)]],
                    axis=0,
                )
                side = 0.1 * (dot(be_m[...], side_in) + dot(halo[near, zs, win(j)], sy_m[kind[j]]))
                dst[:, cols(j)] = (side * one(there)).astype(jnp.bfloat16)

    def slopes(zb):
        own = (zb * ZB + 1) * rows
        for j in range(blocks):
            near = jnp.concatenate(
                [sm[own : own + m, cols(j)], slo[:, cols(j)], shi[:, cols(j)]], axis=0
            )
            gx[:, cols(j)] = dot(dx_m[...], near)
            gy[:, cols(j)] = dot(sm[own : own + m, win(j)], dy_m[kind[j]])

    part = width // depths
    halves = rows // 8
    lanes = part // 128
    step = 4
    zero = jnp.zeros((8, 128), jnp.float32)

    def composite(zb, row, col, n):
        def spot(z):
            return pl.ds(pl.multiple_of(z * rows + row, 8), 8)

        def march(i, state):
            prev, here, tau, through, total, line, *bends = state
            for u in range(step):
                z = i * step + u
                after = sf[spot(zb * ZB + z + 2), col]
                sx, sy = gx[spot(z), col], gy[spot(z), col]
                sz = after - prev
                facing = jnp.abs(0.42 * sz + 0.56 * sx)
                shading = 0.3 + facing * lax.rsqrt(sz * sz + sx * sx + (sy * sy + 0.4))
                x = jnp.minimum(jnp.maximum(here, tab[0]), tab[count - 1])
                tops = [jnp.maximum(x, tab[k]) for k in range(1, count - 1)]
                terms = [tab[5 * count - 1] + tab[4 * count] * x]
                terms += [tab[4 * count + k] * tops[k - 1] for k in range(1, count - 1)]
                while len(terms) > 1:
                    terms = [
                        terms[q] + terms[q + 1] if q + 1 < len(terms) else terms[q]
                        for q in range(0, len(terms), 2)
                    ]
                tau = tau + terms[0]
                left = jnp.exp2(tau)
                weight = shading * (through - left)
                through = left
                total = total + weight
                line = line + weight * x
                bends = [bends[k] + weight * tops[k] for k in range(count - 2)]
                prev, here = here, after
            return (prev, here, tau, through, total, line, *bends)

        state = (sf[spot(zb * ZB), col], sf[spot(zb * ZB + 1), col])
        if zb == 0:
            state += (zero, zero + 1.0) + (zero,) * count
        else:
            state += tuple(sums[n, k] for k in range(count + 2))
        return lax.fori_loop(0, ZB // step, march, state)[2:]

    def middle(zb):
        def piece(p, carry):
            row = pl.multiple_of(lax.rem(p, halves) * 8, 8)
            col = pl.ds(pl.multiple_of((p // halves) * 128, 128), 128)
            state = composite(zb, row, col, p)
            for k in range(count + 2):
                sums[p, k] = state[k]
            return carry

        lax.fori_loop(0, halves * (width // 128), piece, 0)

    def finish(i, carry):
        whose = lax.rem(d + 1 + i, depths)

        def piece(p, carry):
            row = pl.multiple_of(lax.rem(p, halves) * 8, 8)
            place = pl.multiple_of((p // halves) * 128, 128)
            col = pl.ds(pl.multiple_of(whose * part + place, 128), 128)
            tau, _, total, line, *bends = composite(
                groups - 1, row, col, whose * halves * lanes + p
            )
            for c in range(3):
                value = tab[count * (c + 2) - 1] * total + tab[count * (c + 1)] * line
                for k in range(1, count - 1):
                    value = value + tab[count * (c + 1) + k] * bends[k - 1]
                stage[whose, c, pl.ds(row, 8), pl.ds(place, 128)] = value
            stage[whose, 3, pl.ds(row, 8), pl.ds(place, 128)] = tau
            return carry

        lax.fori_loop(0, halves * lanes, piece, 0)

        @pl.when(i < depths - 1)
        def _():
            remote(stage.at[whose], parts.at[d], f_send.at[i], f_recv.at[i], whose, t).start()

        return carry

    arrived(z_copies)
    arrived(x_copies[:2])
    smooth(0)
    arrived(c_copies)
    edge(0, 0, 0, nearer)
    for zb in range(groups):
        if zb < groups - 1:
            arrived(x_copies[2 * zb + 2 : 2 * zb + 4])
            smooth(zb + 1)
        else:
            edge((planes + 1) * rows, (planes + 1) * rows, 2 * ZB, farther)
        sides(zb)
        slopes(zb)
        if zb < groups - 1:
            middle(zb)
        else:
            lax.fori_loop(0, depths, finish, 0)

    parts[d] = stage[d]
    for i in range(depths - 1):
        whose = lax.rem(d + 1 + i, depths)
        source = lax.rem(d - 1 - i + depths, depths)
        remote(stage.at[whose], parts.at[source], f_send.at[i], f_recv.at[i], whose, t).wait_recv()

    for row in range(0, rows, 8):
        for place in range(0, part, 128):
            spots = (slice(row, row + 8), slice(place, place + 128))
            ahead = parts[(0, 3) + spots]
            colors = [parts[(0, c) + spots] for c in range(3)]
            for i in range(1, depths):
                left = jnp.exp2(ahead)
                colors = [colors[c] + left * parts[(i, c) + spots] for c in range(3)]
                ahead = ahead + parts[(i, 3) + spots]
            for c in range(3):
                out[(c,) + spots] = colors[c]
            out[(3,) + spots] = 1.0 - jnp.exp2(ahead)

    for copy, sends, receives, target in z_copies + x_copies + c_copies:
        pl.when(sends)(copy.wait_send)
    for i in range(depths - 1):
        whose = lax.rem(d + 1 + i, depths)
        remote(stage.at[whose], parts.at[d], f_send.at[i], f_recv.at[i], whose, t).wait_send()


def solution(mesh):
    sizes = (mesh.shape["depth"], mesh.shape["tile"])

    def body(volume, knot_pos, knot_color):
        planes, rows, width = volume.shape
        consts = [jnp.asarray(c) for c in constants(planes, rows, width)]
        part = width // sizes[0]
        bf, f32 = jnp.bfloat16, jnp.float32
        dma = pltpu.SemaphoreType.DMA
        smem = pl.BlockSpec(memory_space=pltpu.SMEM)
        anywhere = pl.BlockSpec(memory_space=pltpu.HBM)
        return pl.pallas_call(
            functools.partial(compute, sizes),
            out_shape=jax.ShapeDtypeStruct((4, rows, part), f32),
            in_specs=[smem, smem] + [anywhere] * (1 + len(consts)),
            out_specs=pl.BlockSpec(memory_space=pltpu.VMEM),
            scratch_shapes=[
                pltpu.VMEM(((planes + 4) * rows, width), bf),
                pltpu.VMEM((4, planes, width), bf),
                pltpu.VMEM((2, planes, width), bf),
                pltpu.VMEM((2, planes, width), bf),
                pltpu.VMEM((4 * ZB, width), bf),
                pltpu.VMEM(((planes + 2) * rows, width), bf),
                pltpu.VMEM((ZB, width), bf),
                pltpu.VMEM((ZB, width), bf),
                pltpu.VMEM(((planes + 2) * rows, width), f32),
                pltpu.VMEM((ZB * rows, width), f32),
                pltpu.VMEM((ZB * rows, width), f32),
                pltpu.VMEM((5 * knot_pos.shape[0], 8, 128), f32),
                pltpu.VMEM((sizes[0], 4, rows, part), f32),
                pltpu.VMEM((sizes[0], 4, rows, part), f32),
                pltpu.VMEM((rows // 8 * (width // 128), knot_pos.shape[0] + 2, 8, 128), f32),
            ]
            + [pltpu.VMEM(c.shape, c.dtype) for c in consts]
            + [
                dma((planes // ZB,)), dma((len(consts),)),
                dma((2,)), dma((2,)),
                dma((2 * planes // ZB,)), dma((2 * planes // ZB,)),
                dma((4,)), dma((4,)),
                dma((sizes[0] - 1,)), dma((sizes[0] - 1,)),
            ],
            compiler_params=pltpu.CompilerParams(
                vmem_limit_bytes=62 << 20, collective_id=0, has_side_effects=True
            ),
        )(knot_pos, knot_color, volume.reshape(planes * rows, width), *consts)

    in_specs = (P("depth", "tile", None), P(), P())
    return jax.shard_map(
        body, mesh=mesh, in_specs=in_specs, out_specs=P(None, "tile", "depth"), check_vma=False
    )
```

```python
import functools
import math

import jax
import jax.numpy as jnp
import numpy as np
from jax import lax
from jax.experimental import pallas as pl
from jax.experimental.pallas import tpu as pltpu
from jax.sharding import PartitionSpec as P

ZB = 16
CB = 256


def windows(width):
    last = width - 2 * CB
    return [min(max(j * CB - CB // 2, 0), last) for j in range(width // CB)]


def along_y(width, before, after):
    mats, index = [], []
    for j, start in enumerate(windows(width)):
        offset = j * CB - start
        if offset not in index:
            index.append(offset)
            k = np.arange(2 * CB)[:, None] - offset
            n = np.arange(CB)[None, :]
            mats.append(before * (k == n - 1) + after * (k == n + 1))
    return np.stack(mats).astype(jnp.bfloat16)


def window_kind(width):
    kinds = []
    out = []
    for j, start in enumerate(windows(width)):
        offset = j * CB - start
        if offset not in kinds:
            kinds.append(offset)
        out.append(kinds.index(offset))
    return out


def constants(planes, rows, width):
    m = ZB * rows
    a = np.zeros((m, m + 2 * rows + 2 * ZB), np.float32)
    dx = np.zeros((m, m + 2 * ZB), np.float32)
    for z in range(ZB):
        for x in range(rows):
            o = z * rows + x
            c = o + rows
            a[o, c] += 4
            a[o, c - rows] += 1
            a[o, c + rows] += 1
            a[o, c - 1 if x else m + 2 * rows + z] += 1
            a[o, c + 1 if x < rows - 1 else m + 2 * rows + ZB + z] += 1
            dx[o, o - 1 if x else m + z] -= 1
            dx[o, o + 1 if x < rows - 1 else m + ZB + z] += 1
    ae = np.zeros((2, rows, 3 * rows + 2 * ZB), np.float32)
    for e in range(2):
        beside = 0 if e else ZB - 1
        for x in range(rows):
            c = rows + x
            ae[e, x, c] += 4
            ae[e, x, c - rows] += 1
            ae[e, x, c + rows] += 1
            ae[e, x, c - 1 if x else 3 * rows + beside] += 1
            ae[e, x, c + 1 if x < rows - 1 else 3 * rows + ZB + beside] += 1
    be = np.zeros((ZB, 5 * ZB), np.float32)
    for z in range(ZB):
        be[z, ZB + z] += 4
        be[z, ZB + z - 1] += 1
        be[z, ZB + z + 1] += 1
        be[z, 3 * ZB + z] += 1
        be[z, 4 * ZB + z] += 1
    pack = np.zeros((4 * ZB, m), np.float32)
    for r, row in enumerate((0, 1, rows - 2, rows - 1)):
        for z in range(ZB):
            pack[r * ZB + z, z * rows + row] = 1
    bf = lambda t: t.astype(jnp.bfloat16)
    return [bf(pack), along_y(width, 1, 1), bf(a), bf(ae), bf(be), bf(dx), along_y(width, -1, 1)]


def dot(a, b):
    return jnp.dot(a, b, preferred_element_type=jnp.float32)


def compute(
    sizes, knot_pos, knot_color, vol,
    pack_h, sy_h, a_h, ae_h, be_h, dx_h, dy_h,
    out, field, packed, hlo, hhi, corners, sm, slo, shi, sf, gx, gy, tab, stage, parts, sums,
    pack_m, sy_m, a_m, ae_m, be_m, dx_m, dy_m,
    vol_sem, const_sem, z_send, z_recv, x_send, x_recv, c_send, c_recv, f_send, f_recv,
):
    rows, width = out.shape[1], vol.shape[1]
    planes = vol.shape[0] // rows
    depths, tiles = sizes
    d, t = lax.axis_index("depth"), lax.axis_index("tile")
    kind, starts = window_kind(width), windows(width)
    blocks = len(starts)
    groups = planes // ZB
    m = ZB * rows
    count = knot_pos.shape[0]

    loads = []
    for zb in range(groups):
        loads.append(
            pltpu.make_async_copy(
                vol.at[pl.ds(zb * m, m)],
                field.at[pl.ds(2 * rows + zb * m, m)],
                vol_sem.at[zb],
            )
        )
    fetches = [
        pltpu.make_async_copy(src, dst, const_sem.at[i])
        for i, (src, dst) in enumerate(
            (
                (pack_h, pack_m), (sy_h, sy_m), (a_h, a_m), (ae_h, ae_m),
                (be_h, be_m), (dx_h, dx_m), (dy_h, dy_m),
            )
        )
    ]
    fetches[0].start()
    for copy in loads + fetches[1:]:
        copy.start()

    barrier = pltpu.get_barrier_semaphore()

    def hello(depth, tile):
        pl.semaphore_signal(
            barrier, inc=1, device_id=(depth, tile), device_id_type=pl.DeviceIdType.MESH
        )

    lower, upper = t > 0, t < tiles - 1
    nearer, farther = d > 0, d < depths - 1
    near_d, far_d = jnp.maximum(d - 1, 0), jnp.minimum(d + 1, depths - 1)
    low_t, up_t = jnp.maximum(t - 1, 0), jnp.minimum(t + 1, tiles - 1)
    for k in range(1, depths):
        hello(lax.rem(d + k, depths), t)
    for there, tile in ((lower, low_t), (upper, up_t)):
        pl.when(there)(functools.partial(hello, d, tile))
        pl.when(there & nearer)(functools.partial(hello, near_d, tile))
        pl.when(there & farther)(functools.partial(hello, far_d, tile))
    number = lambda flag: jnp.where(flag, 1, 0)
    greeted = (depths - 1) + (number(lower) + number(upper)) * (
        1 + number(nearer) + number(farther)
    )

    def splat(value):
        return jnp.full((8, 128), value, jnp.int32).astype(jnp.float32)

    at = [(splat(knot_pos[k]) - 127.5) * (1.0 / 70.0) for k in range(count)]
    gaps = [1.0 / (at[k + 1] - at[k]) for k in range(count - 1)]
    for k in range(count):
        tab[k] = at[k]
    scales = [1 / 255.0] * 3 + [-4.0 * math.log2(math.e) / (planes * depths) / 255.0]
    for c in range(4):
        value = [splat(knot_color[c, k]) * scales[c] for k in range(count)]
        const, before = value[0], None
        for k in range(count - 1):
            slope = (value[k + 1] - value[k]) * gaps[k]
            bend = slope if k == 0 else slope - before
            before = slope
            const = const - bend * at[k]
            tab[count * (c + 1) + k] = bend
        tab[count * (c + 1) + count - 1] = const

    def cols(j):
        return slice(j * CB, (j + 1) * CB)

    def win(j):
        return slice(starts[j], starts[j] + 2 * CB)

    fetches[0].wait()
    for zb in range(groups):
        loads[zb].wait()
        for j in range(blocks):
            picked = dot(pack_m[...], field[2 * rows + zb * m : 2 * rows + (zb + 1) * m, cols(j)])
            picked = picked.astype(jnp.bfloat16)
            for r in range(4):
                packed[r, zb * ZB : (zb + 1) * ZB, cols(j)] = picked[r * ZB : (r + 1) * ZB]

    pl.semaphore_wait(barrier, greeted)

    def remote(src, dst, send, recv, depth, tile):
        return pltpu.make_async_remote_copy(
            src_ref=src, dst_ref=dst, send_sem=send, recv_sem=recv,
            device_id=(depth, tile), device_id_type=pl.DeviceIdType.MESH,
        )

    inside, end = 2 * rows, (planes + 2) * rows
    z_copies, x_copies, c_copies = [], [], []
    for i, (src, dst, depth, sends, receives) in enumerate(
        (
            (end - 2 * rows, 0, far_d, farther, nearer),
            (inside, end, near_d, nearer, farther),
        )
    ):
        target = field.at[pl.ds(dst, 2 * rows)]
        z_copies.append(
            (
                remote(
                    field.at[pl.ds(src, 2 * rows)], target,
                    z_send.at[i], z_recv.at[i], depth, t,
                ),
                sends, receives, target,
            )
        )
    for zb in range(groups):
        zs = pl.ds(zb * ZB, ZB)
        for i, (src, halo, tile, sends, receives) in enumerate(
            ((2, hlo, up_t, upper, lower), (0, hhi, low_t, lower, upper))
        ):
            target = halo.at[:, zs]
            n = 2 * zb + i
            x_copies.append(
                (
                    remote(
                        packed.at[pl.ds(src, 2), zs], target,
                        x_send.at[n], x_recv.at[n], d, tile,
                    ),
                    sends, receives, target,
                )
            )
    for i, (row, z, depth, tile, sends, receives) in enumerate(
        (
            (3, planes - ZB, far_d, up_t, farther & upper, nearer & lower),
            (0, planes - ZB, far_d, low_t, farther & lower, nearer & upper),
            (3, 0, near_d, up_t, nearer & upper, farther & lower),
            (0, 0, near_d, low_t, nearer & lower, farther & upper),
        )
    ):
        target = corners.at[pl.ds(i * ZB, ZB)]
        c_copies.append(
            (
                remote(
                    packed.at[row, pl.ds(z, ZB)], target,
                    c_send.at[i], c_recv.at[i], depth, tile,
                ),
                sends, receives, target,
            )
        )
    def depart(copies):
        for copy, sends, receives, target in copies:
            pl.when(sends)(copy.start)

    depart(x_copies[:2] + z_copies + c_copies[:2] + x_copies[2:4])

    for copy, sends, receives, target in z_copies + x_copies + c_copies:

        @pl.when(jnp.logical_not(receives))
        def _():
            target[...] = jnp.zeros(target.shape, jnp.bfloat16)

    def arrived(copies):
        for copy, sends, receives, target in copies:
            pl.when(receives)(copy.wait_recv)

    for copy in fetches[1:]:
        copy.wait()

    def smooth(zb):
        first, own = (zb * ZB + 1) * rows, (zb * ZB + 2) * rows
        zs = slice(zb * ZB, (zb + 1) * ZB)
        for j in range(blocks):
            near = jnp.concatenate(
                [field[first : first + m + 2 * rows, cols(j)], hlo[1, zs, cols(j)], hhi[0, zs, cols(j)]],
                axis=0,
            )
            value = dot(a_m[...], near) + dot(field[own : own + m, win(j)], sy_m[kind[j]])
            rounded = (0.1 * value).astype(jnp.bfloat16)
            sm[first : first + m, cols(j)] = rounded
            sf[first : first + m, cols(j)] = rounded.astype(jnp.float32)

    one = lambda flag: jnp.where(flag, 1.0, 0.0)

    def edge(first, put, corner, there):
        for j in range(blocks):
            near = jnp.concatenate(
                [field[first : first + 3 * rows, cols(j)], corners[corner : corner + 2 * ZB, cols(j)]],
                axis=0,
            )
            own = field[first + rows : first + 2 * rows, win(j)]
            value = 0.1 * (dot(ae_m[corner // (2 * ZB)], near) + dot(own, sy_m[kind[j]]))
            value = (value * one(there)).astype(jnp.bfloat16)
            sf[put : put + rows, cols(j)] = value.astype(jnp.float32)

    def sides(zb):
        zs = slice(zb * ZB, (zb + 1) * ZB)
        for j in range(blocks):
            for s, (halo, near, far, own, dst, there) in enumerate(
                ((hlo, 1, 0, 0, slo, lower), (hhi, 0, 1, 3, shi, upper))
            ):

                def block(b):
                    if b < 0:
                        return corners[s * ZB : (s + 1) * ZB, cols(j)]
                    if b == groups:
                        return corners[(2 + s) * ZB : (3 + s) * ZB, cols(j)]
                    return halo[near, b * ZB : (b + 1) * ZB, cols(j)]

                side_in = jnp.concatenate(
                    [block(zb - 1), block(zb), block(zb + 1), halo[far, zs, cols(j)], packed[own, zs, cols(j)]],
                    axis=0,
                )
                side = 0.1 * (dot(be_m[...], side_in) + dot(halo[near, zs, win(j)], sy_m[kind[j]]))
                dst[:, cols(j)] = (side * one(there)).astype(jnp.bfloat16)

    def slopes(zb):
        own = (zb * ZB + 1) * rows
        for j in range(blocks):
            near = jnp.concatenate(
                [sm[own : own + m, cols(j)], slo[:, cols(j)], shi[:, cols(j)]], axis=0
            )
            gx[:, cols(j)] = dot(dx_m[...], near)
            gy[:, cols(j)] = dot(sm[own : own + m, win(j)], dy_m[kind[j]])

    part = width // depths
    halves = rows // 8
    lanes = part // 128
    step = 4
    zero = jnp.zeros((8, 128), jnp.float32)

    def composite(zb, row, col, n):
        def spot(z):
            return pl.ds(pl.multiple_of(z * rows + row, 8), 8)

        def march(i, state):
            prev, here, tau, through, total, line, *bends = state
            for u in range(step):
                z = i * step + u
                after = sf[spot(zb * ZB + z + 2), col]
                sx, sy = gx[spot(z), col], gy[spot(z), col]
                sz = after - prev
                facing = jnp.abs(0.42 * sz + 0.56 * sx)
                shading = 0.3 + facing * lax.rsqrt(sz * sz + sx * sx + (sy * sy + 0.4))
                x = jnp.minimum(jnp.maximum(here, tab[0]), tab[count - 1])
                tops = [jnp.maximum(x, tab[k]) for k in range(1, count - 1)]
                terms = [tab[5 * count - 1] + tab[4 * count] * x]
                terms += [tab[4 * count + k] * tops[k - 1] for k in range(1, count - 1)]
                while len(terms) > 1:
                    terms = [
                        terms[q] + terms[q + 1] if q + 1 < len(terms) else terms[q]
                        for q in range(0, len(terms), 2)
                    ]
                tau = tau + terms[0]
                left = jnp.exp2(tau)
                weight = shading * (through - left)
                through = left
                total = total + weight
                line = line + weight * x
                bends = [bends[k] + weight * tops[k] for k in range(count - 2)]
                prev, here = here, after
            return (prev, here, tau, through, total, line, *bends)

        state = (sf[spot(zb * ZB), col], sf[spot(zb * ZB + 1), col])
        if zb == 0:
            state += (zero, zero + 1.0) + (zero,) * count
        else:
            state += tuple(sums[n, k] for k in range(count + 2))
        return lax.fori_loop(0, ZB // step, march, state)[2:]

    def middle(zb):
        def piece(p, carry):
            row = pl.multiple_of(lax.rem(p, halves) * 8, 8)
            col = pl.ds(pl.multiple_of((p // halves) * 128, 128), 128)
            state = composite(zb, row, col, p)
            for k in range(count + 2):
                sums[p, k] = state[k]
            return carry

        lax.fori_loop(0, halves * (width // 128), piece, 0)

    def finish(i, carry):
        whose = lax.rem(d + 1 + i, depths)

        def piece(p, carry):
            row = pl.multiple_of(lax.rem(p, halves) * 8, 8)
            place = pl.multiple_of((p // halves) * 128, 128)
            col = pl.ds(pl.multiple_of(whose * part + place, 128), 128)
            tau, _, total, line, *bends = composite(
                groups - 1, row, col, whose * halves * lanes + p
            )
            for c in range(3):
                value = tab[count * (c + 2) - 1] * total + tab[count * (c + 1)] * line
                for k in range(1, count - 1):
                    value = value + tab[count * (c + 1) + k] * bends[k - 1]
                stage[whose, c, pl.ds(row, 8), pl.ds(place, 128)] = value
            stage[whose, 3, pl.ds(row, 8), pl.ds(place, 128)] = tau
            return carry

        lax.fori_loop(0, halves * lanes, piece, 0)

        @pl.when(i < depths - 1)
        def _():
            remote(stage.at[whose], parts.at[d], f_send.at[i], f_recv.at[i], whose, t).start()

        return carry

    arrived(z_copies[:1])
    arrived(x_copies[:2])
    smooth(0)
    arrived(c_copies[:2])
    edge(0, 0, 0, nearer)
    for zb in range(groups):
        if zb < groups - 1:
            arrived(x_copies[2 * zb + 2 : 2 * zb + 4])
            if zb == 0:
                depart(x_copies[4:] + c_copies[2:])
            if zb == groups - 2:
                arrived(z_copies[1:])
            smooth(zb + 1)
        else:
            arrived(c_copies[2:])
            edge((planes + 1) * rows, (planes + 1) * rows, 2 * ZB, farther)
        sides(zb)
        slopes(zb)
        if zb < groups - 1:
            middle(zb)
        else:
            lax.fori_loop(0, depths, finish, 0)

    parts[d] = stage[d]
    for i in range(depths - 1):
        whose = lax.rem(d + 1 + i, depths)
        source = lax.rem(d - 1 - i + depths, depths)
        remote(stage.at[whose], parts.at[source], f_send.at[i], f_recv.at[i], whose, t).wait_recv()

    for row in range(0, rows, 8):
        for place in range(0, part, 128):
            spots = (slice(row, row + 8), slice(place, place + 128))
            ahead = parts[(0, 3) + spots]
            colors = [parts[(0, c) + spots] for c in range(3)]
            for i in range(1, depths):
                left = jnp.exp2(ahead)
                colors = [colors[c] + left * parts[(i, c) + spots] for c in range(3)]
                ahead = ahead + parts[(i, 3) + spots]
            for c in range(3):
                out[(c,) + spots] = colors[c]
            out[(3,) + spots] = 1.0 - jnp.exp2(ahead)

    for copy, sends, receives, target in z_copies + x_copies + c_copies:
        pl.when(sends)(copy.wait_send)
    for i in range(depths - 1):
        whose = lax.rem(d + 1 + i, depths)
        remote(stage.at[whose], parts.at[d], f_send.at[i], f_recv.at[i], whose, t).wait_send()


def solution(mesh):
    sizes = (mesh.shape["depth"], mesh.shape["tile"])

    def body(volume, knot_pos, knot_color):
        planes, rows, width = volume.shape
        consts = [jnp.asarray(c) for c in constants(planes, rows, width)]
        part = width // sizes[0]
        bf, f32 = jnp.bfloat16, jnp.float32
        dma = pltpu.SemaphoreType.DMA
        smem = pl.BlockSpec(memory_space=pltpu.SMEM)
        anywhere = pl.BlockSpec(memory_space=pltpu.HBM)
        return pl.pallas_call(
            functools.partial(compute, sizes),
            out_shape=jax.ShapeDtypeStruct((4, rows, part), f32),
            in_specs=[smem, smem] + [anywhere] * (1 + len(consts)),
            out_specs=pl.BlockSpec(memory_space=pltpu.VMEM),
            scratch_shapes=[
                pltpu.VMEM(((planes + 4) * rows, width), bf),
                pltpu.VMEM((4, planes, width), bf),
                pltpu.VMEM((2, planes, width), bf),
                pltpu.VMEM((2, planes, width), bf),
                pltpu.VMEM((4 * ZB, width), bf),
                pltpu.VMEM(((planes + 2) * rows, width), bf),
                pltpu.VMEM((ZB, width), bf),
                pltpu.VMEM((ZB, width), bf),
                pltpu.VMEM(((planes + 2) * rows, width), f32),
                pltpu.VMEM((ZB * rows, width), f32),
                pltpu.VMEM((ZB * rows, width), f32),
                pltpu.VMEM((5 * knot_pos.shape[0], 8, 128), f32),
                pltpu.VMEM((sizes[0], 4, rows, part), f32),
                pltpu.VMEM((sizes[0], 4, rows, part), f32),
                pltpu.VMEM((rows // 8 * (width // 128), knot_pos.shape[0] + 2, 8, 128), f32),
            ]
            + [pltpu.VMEM(c.shape, c.dtype) for c in consts]
            + [
                dma((planes // ZB,)), dma((len(consts),)),
                dma((2,)), dma((2,)),
                dma((2 * planes // ZB,)), dma((2 * planes // ZB,)),
                dma((4,)), dma((4,)),
                dma((sizes[0] - 1,)), dma((sizes[0] - 1,)),
            ],
            compiler_params=pltpu.CompilerParams(
                vmem_limit_bytes=62 << 20, collective_id=0, has_side_effects=True
            ),
        )(knot_pos, knot_color, volume.reshape(planes * rows, width), *consts)

    in_specs = (P("depth", "tile", None), P(), P())
    return jax.shard_map(
        body, mesh=mesh, in_specs=in_specs, out_specs=P(None, "tile", "depth"), check_vma=False
    )
```

```python
import functools
import math

import jax
import jax.numpy as jnp
import numpy as np
from jax import lax
from jax.experimental import pallas as pl
from jax.experimental.pallas import tpu as pltpu
from jax.sharding import PartitionSpec as P

ZB = 16
CB = 256


def windows(width):
    last = width - 2 * CB
    return [min(max(j * CB - CB // 2, 0), last) for j in range(width // CB)]


def along_y(width, before, after):
    mats, index = [], []
    for j, start in enumerate(windows(width)):
        offset = j * CB - start
        if offset not in index:
            index.append(offset)
            k = np.arange(2 * CB)[:, None] - offset
            n = np.arange(CB)[None, :]
            mats.append(before * (k == n - 1) + after * (k == n + 1))
    return np.stack(mats).astype(jnp.bfloat16)


def window_kind(width):
    kinds = []
    out = []
    for j, start in enumerate(windows(width)):
        offset = j * CB - start
        if offset not in kinds:
            kinds.append(offset)
        out.append(kinds.index(offset))
    return out


def constants(planes, rows, width):
    m = ZB * rows
    a = np.zeros((m, m + 2 * rows + 2 * ZB), np.float32)
    dx = np.zeros((m, m + 2 * ZB), np.float32)
    for z in range(ZB):
        for x in range(rows):
            o = z * rows + x
            c = o + rows
            a[o, c] += 4
            a[o, c - rows] += 1
            a[o, c + rows] += 1
            a[o, c - 1 if x else m + 2 * rows + z] += 1
            a[o, c + 1 if x < rows - 1 else m + 2 * rows + ZB + z] += 1
            dx[o, o - 1 if x else m + z] -= 1
            dx[o, o + 1 if x < rows - 1 else m + ZB + z] += 1
    ae = np.zeros((2, rows, 3 * rows + 2 * ZB), np.float32)
    for e in range(2):
        beside = 0 if e else ZB - 1
        for x in range(rows):
            c = rows + x
            ae[e, x, c] += 4
            ae[e, x, c - rows] += 1
            ae[e, x, c + rows] += 1
            ae[e, x, c - 1 if x else 3 * rows + beside] += 1
            ae[e, x, c + 1 if x < rows - 1 else 3 * rows + ZB + beside] += 1
    be = np.zeros((ZB, 5 * ZB), np.float32)
    for z in range(ZB):
        be[z, ZB + z] += 4
        be[z, ZB + z - 1] += 1
        be[z, ZB + z + 1] += 1
        be[z, 3 * ZB + z] += 1
        be[z, 4 * ZB + z] += 1
    pack = np.zeros((4 * ZB, m), np.float32)
    for r, row in enumerate((0, 1, rows - 2, rows - 1)):
        for z in range(ZB):
            pack[r * ZB + z, z * rows + row] = 1
    bf = lambda t: t.astype(jnp.bfloat16)
    return [bf(pack), along_y(width, 1, 1), bf(a), bf(ae), bf(be), bf(dx), along_y(width, -1, 1)]


def dot(a, b):
    return jnp.dot(a, b, preferred_element_type=jnp.float32)


def compute(
    sizes, knot_pos, knot_color, vol,
    pack_h, sy_h, a_h, ae_h, be_h, dx_h, dy_h,
    out, field, packed, hlo, hhi, corners, sm, slo, shi, sf, gx, gy, tab, stage, parts, sums,
    pack_m, sy_m, a_m, ae_m, be_m, dx_m, dy_m,
    vol_sem, const_sem, z_send, z_recv, x_send, x_recv, c_send, c_recv, f_send, f_recv,
):
    rows, width = out.shape[1], vol.shape[1]
    planes = vol.shape[0] // rows
    depths, tiles = sizes
    d, t = lax.axis_index("depth"), lax.axis_index("tile")
    kind, starts = window_kind(width), windows(width)
    blocks = len(starts)
    groups = planes // ZB
    m = ZB * rows
    count = knot_pos.shape[0]

    loads = []
    for zb in range(groups):
        loads.append(
            pltpu.make_async_copy(
                vol.at[pl.ds(zb * m, m)],
                field.at[pl.ds(2 * rows + zb * m, m)],
                vol_sem.at[zb],
            )
        )
    fetches = [
        pltpu.make_async_copy(src, dst, const_sem.at[i])
        for i, (src, dst) in enumerate(
            (
                (pack_h, pack_m), (sy_h, sy_m), (a_h, a_m), (ae_h, ae_m),
                (be_h, be_m), (dx_h, dx_m), (dy_h, dy_m),
            )
        )
    ]
    fetches[0].start()
    for copy in loads + fetches[1:]:
        copy.start()

    barrier = pltpu.get_barrier_semaphore()

    def hello(depth, tile):
        pl.semaphore_signal(
            barrier, inc=1, device_id=(depth, tile), device_id_type=pl.DeviceIdType.MESH
        )

    lower, upper = t > 0, t < tiles - 1
    nearer, farther = d > 0, d < depths - 1
    near_d, far_d = jnp.maximum(d - 1, 0), jnp.minimum(d + 1, depths - 1)
    low_t, up_t = jnp.maximum(t - 1, 0), jnp.minimum(t + 1, tiles - 1)
    for k in range(1, depths):
        hello(lax.rem(d + k, depths), t)
    for there, tile in ((lower, low_t), (upper, up_t)):
        pl.when(there)(functools.partial(hello, d, tile))
        pl.when(there & nearer)(functools.partial(hello, near_d, tile))
        pl.when(there & farther)(functools.partial(hello, far_d, tile))
    number = lambda flag: jnp.where(flag, 1, 0)
    greeted = (depths - 1) + (number(lower) + number(upper)) * (
        1 + number(nearer) + number(farther)
    )

    def splat(value):
        return jnp.full((8, 128), value, jnp.int32).astype(jnp.float32)

    at = [(splat(knot_pos[k]) - 127.5) * (1.0 / 70.0) for k in range(count)]
    gaps = [1.0 / (at[k + 1] - at[k]) for k in range(count - 1)]
    for k in range(count):
        tab[k] = at[k]
    scales = [1 / 255.0] * 3 + [-4.0 * math.log2(math.e) / (planes * depths) / 255.0]
    for c in range(4):
        value = [splat(knot_color[c, k]) * scales[c] for k in range(count)]
        const, before = value[0], None
        for k in range(count - 1):
            slope = (value[k + 1] - value[k]) * gaps[k]
            bend = slope if k == 0 else slope - before
            before = slope
            const = const - bend * at[k]
            tab[count * (c + 1) + k] = bend
        tab[count * (c + 1) + count - 1] = const

    def cols(j):
        return slice(j * CB, (j + 1) * CB)

    def win(j):
        return slice(starts[j], starts[j] + 2 * CB)

    fetches[0].wait()
    for zb in range(groups):
        loads[zb].wait()
        for j in range(blocks):
            picked = dot(pack_m[...], field[2 * rows + zb * m : 2 * rows + (zb + 1) * m, cols(j)])
            picked = picked.astype(jnp.bfloat16)
            for r in range(4):
                packed[r, zb * ZB : (zb + 1) * ZB, cols(j)] = picked[r * ZB : (r + 1) * ZB]

    pl.semaphore_wait(barrier, greeted)

    def remote(src, dst, send, recv, depth, tile):
        return pltpu.make_async_remote_copy(
            src_ref=src, dst_ref=dst, send_sem=send, recv_sem=recv,
            device_id=(depth, tile), device_id_type=pl.DeviceIdType.MESH,
        )

    inside, end = 2 * rows, (planes + 2) * rows
    z_copies, x_copies, c_copies = [], [], []
    for i, (src, dst, depth, sends, receives) in enumerate(
        (
            (end - 2 * rows, 0, far_d, farther, nearer),
            (inside, end, near_d, nearer, farther),
        )
    ):
        target = field.at[pl.ds(dst, 2 * rows)]
        z_copies.append(
            (
                remote(
                    field.at[pl.ds(src, 2 * rows)], target,
                    z_send.at[i], z_recv.at[i], depth, t,
                ),
                sends, receives, target,
            )
        )
    for zb in range(groups):
        zs = pl.ds(zb * ZB, ZB)
        for i, (src, halo, tile, sends, receives) in enumerate(
            ((2, hlo, up_t, upper, lower), (0, hhi, low_t, lower, upper))
        ):
            target = halo.at[:, zs]
            n = 2 * zb + i
            x_copies.append(
                (
                    remote(
                        packed.at[pl.ds(src, 2), zs], target,
                        x_send.at[n], x_recv.at[n], d, tile,
                    ),
                    sends, receives, target,
                )
            )
    for i, (row, z, depth, tile, sends, receives) in enumerate(
        (
            (3, planes - ZB, far_d, up_t, farther & upper, nearer & lower),
            (0, planes - ZB, far_d, low_t, farther & lower, nearer & upper),
            (3, 0, near_d, up_t, nearer & upper, farther & lower),
            (0, 0, near_d, low_t, nearer & lower, farther & upper),
        )
    ):
        target = corners.at[pl.ds(i * ZB, ZB)]
        c_copies.append(
            (
                remote(
                    packed.at[row, pl.ds(z, ZB)], target,
                    c_send.at[i], c_recv.at[i], depth, tile,
                ),
                sends, receives, target,
            )
        )
    def depart(copies):
        for copy, sends, receives, target in copies:
            pl.when(sends)(copy.start)

    depart(x_copies[:2] + z_copies + c_copies[:2] + x_copies[2:4])

    for copy, sends, receives, target in z_copies + x_copies + c_copies:

        @pl.when(jnp.logical_not(receives))
        def _():
            target[...] = jnp.zeros(target.shape, jnp.bfloat16)

    def arrived(copies):
        for copy, sends, receives, target in copies:
            pl.when(receives)(copy.wait_recv)

    for copy in fetches[1:]:
        copy.wait()

    def smooth(zb):
        first, own = (zb * ZB + 1) * rows, (zb * ZB + 2) * rows
        zs = slice(zb * ZB, (zb + 1) * ZB)
        for j in range(blocks):
            near = jnp.concatenate(
                [field[first : first + m + 2 * rows, cols(j)], hlo[1, zs, cols(j)], hhi[0, zs, cols(j)]],
                axis=0,
            )
            value = dot(a_m[...], near) + dot(field[own : own + m, win(j)], sy_m[kind[j]])
            rounded = (0.1 * value).astype(jnp.bfloat16)
            sm[first : first + m, cols(j)] = rounded
            sf[first : first + m, cols(j)] = rounded.astype(jnp.float32)

    one = lambda flag: jnp.where(flag, 1.0, 0.0)

    def edge(first, put, corner, there):
        for j in range(blocks):
            near = jnp.concatenate(
                [field[first : first + 3 * rows, cols(j)], corners[corner : corner + 2 * ZB, cols(j)]],
                axis=0,
            )
            own = field[first + rows : first + 2 * rows, win(j)]
            value = 0.1 * (dot(ae_m[corner // (2 * ZB)], near) + dot(own, sy_m[kind[j]]))
            value = (value * one(there)).astype(jnp.bfloat16)
            sf[put : put + rows, cols(j)] = value.astype(jnp.float32)

    def sides(zb):
        zs = slice(zb * ZB, (zb + 1) * ZB)
        for j in range(blocks):
            for s, (halo, near, far, own, dst, there) in enumerate(
                ((hlo, 1, 0, 0, slo, lower), (hhi, 0, 1, 3, shi, upper))
            ):

                def block(b):
                    if b < 0:
                        return corners[s * ZB : (s + 1) * ZB, cols(j)]
                    if b == groups:
                        return corners[(2 + s) * ZB : (3 + s) * ZB, cols(j)]
                    return halo[near, b * ZB : (b + 1) * ZB, cols(j)]

                side_in = jnp.concatenate(
                    [block(zb - 1), block(zb), block(zb + 1), halo[far, zs, cols(j)], packed[own, zs, cols(j)]],
                    axis=0,
                )
                side = 0.1 * (dot(be_m[...], side_in) + dot(halo[near, zs, win(j)], sy_m[kind[j]]))
                dst[:, cols(j)] = (side * one(there)).astype(jnp.bfloat16)

    def slopes(zb):
        own = (zb * ZB + 1) * rows
        for j in range(blocks):
            near = jnp.concatenate(
                [sm[own : own + m, cols(j)], slo[:, cols(j)], shi[:, cols(j)]], axis=0
            )
            gx[:, cols(j)] = dot(dx_m[...], near)
            gy[:, cols(j)] = dot(sm[own : own + m, win(j)], dy_m[kind[j]])

    part = width // depths
    halves = rows // 8
    lanes = part // 128
    step = 8
    zero = jnp.zeros((8, 128), jnp.float32)

    def composite(zb, row, col, n):
        def spot(z):
            return pl.ds(pl.multiple_of(z * rows + row, 8), 8)

        def march(i, state):
            prev, here, tau, through, total, line, *bends = state
            for u in range(step):
                z = i * step + u
                after = sf[spot(zb * ZB + z + 2), col]
                sx, sy = gx[spot(z), col], gy[spot(z), col]
                sz = after - prev
                facing = jnp.abs(0.42 * sz + 0.56 * sx)
                shading = 0.3 + facing * lax.rsqrt(sz * sz + sx * sx + (sy * sy + 0.4))
                x = jnp.minimum(jnp.maximum(here, tab[0]), tab[count - 1])
                tops = [jnp.maximum(x, tab[k]) for k in range(1, count - 1)]
                terms = [tab[5 * count - 1] + tab[4 * count] * x]
                terms += [tab[4 * count + k] * tops[k - 1] for k in range(1, count - 1)]
                while len(terms) > 1:
                    terms = [
                        terms[q] + terms[q + 1] if q + 1 < len(terms) else terms[q]
                        for q in range(0, len(terms), 2)
                    ]
                tau = tau + terms[0]
                left = jnp.exp2(tau)
                weight = shading * (through - left)
                through = left
                total = total + weight
                line = line + weight * x
                bends = [bends[k] + weight * tops[k] for k in range(count - 2)]
                prev, here = here, after
            return (prev, here, tau, through, total, line, *bends)

        state = (sf[spot(zb * ZB), col], sf[spot(zb * ZB + 1), col])
        if zb == 0:
            state += (zero, zero + 1.0) + (zero,) * count
        else:
            state += tuple(sums[n, k] for k in range(count + 2))
        return lax.fori_loop(0, ZB // step, march, state)[2:]

    def middle(zb):
        def piece(p, carry):
            row = pl.multiple_of(lax.rem(p, halves) * 8, 8)
            col = pl.ds(pl.multiple_of((p // halves) * 128, 128), 128)
            state = composite(zb, row, col, p)
            for k in range(count + 2):
                sums[p, k] = state[k]
            return carry

        lax.fori_loop(0, halves * (width // 128), piece, 0)

    def finish(i, carry):
        whose = lax.rem(d + 1 + i, depths)

        def piece(p, carry):
            row = pl.multiple_of(lax.rem(p, halves) * 8, 8)
            place = pl.multiple_of((p // halves) * 128, 128)
            col = pl.ds(pl.multiple_of(whose * part + place, 128), 128)
            tau, _, total, line, *bends = composite(
                groups - 1, row, col, whose * halves * lanes + p
            )
            for c in range(3):
                value = tab[count * (c + 2) - 1] * total + tab[count * (c + 1)] * line
                for k in range(1, count - 1):
                    value = value + tab[count * (c + 1) + k] * bends[k - 1]
                stage[whose, c, pl.ds(row, 8), pl.ds(place, 128)] = value
            stage[whose, 3, pl.ds(row, 8), pl.ds(place, 128)] = tau
            return carry

        lax.fori_loop(0, halves * lanes, piece, 0)

        @pl.when(i < depths - 1)
        def _():
            remote(stage.at[whose], parts.at[d], f_send.at[i], f_recv.at[i], whose, t).start()

        return carry

    arrived(z_copies[:1])
    arrived(x_copies[:2])
    smooth(0)
    arrived(c_copies[:2])
    edge(0, 0, 0, nearer)
    for zb in range(groups):
        if zb < groups - 1:
            arrived(x_copies[2 * zb + 2 : 2 * zb + 4])
            if zb == 0:
                depart(x_copies[4:] + c_copies[2:])
            if zb == groups - 2:
                arrived(z_copies[1:])
            smooth(zb + 1)
        else:
            arrived(c_copies[2:])
            edge((planes + 1) * rows, (planes + 1) * rows, 2 * ZB, farther)
        sides(zb)
        slopes(zb)
        if zb < groups - 1:
            middle(zb)
        else:
            lax.fori_loop(0, depths, finish, 0)

    parts[d] = stage[d]
    for i in range(depths - 1):
        whose = lax.rem(d + 1 + i, depths)
        source = lax.rem(d - 1 - i + depths, depths)
        remote(stage.at[whose], parts.at[source], f_send.at[i], f_recv.at[i], whose, t).wait_recv()

    for row in range(0, rows, 8):
        for place in range(0, part, 128):
            spots = (slice(row, row + 8), slice(place, place + 128))
            ahead = parts[(0, 3) + spots]
            colors = [parts[(0, c) + spots] for c in range(3)]
            for i in range(1, depths):
                left = jnp.exp2(ahead)
                colors = [colors[c] + left * parts[(i, c) + spots] for c in range(3)]
                ahead = ahead + parts[(i, 3) + spots]
            for c in range(3):
                out[(c,) + spots] = colors[c]
            out[(3,) + spots] = 1.0 - jnp.exp2(ahead)

    for copy, sends, receives, target in z_copies + x_copies + c_copies:
        pl.when(sends)(copy.wait_send)
    for i in range(depths - 1):
        whose = lax.rem(d + 1 + i, depths)
        remote(stage.at[whose], parts.at[d], f_send.at[i], f_recv.at[i], whose, t).wait_send()


def solution(mesh):
    sizes = (mesh.shape["depth"], mesh.shape["tile"])

    def body(volume, knot_pos, knot_color):
        planes, rows, width = volume.shape
        consts = [jnp.asarray(c) for c in constants(planes, rows, width)]
        part = width // sizes[0]
        bf, f32 = jnp.bfloat16, jnp.float32
        dma = pltpu.SemaphoreType.DMA
        smem = pl.BlockSpec(memory_space=pltpu.SMEM)
        anywhere = pl.BlockSpec(memory_space=pltpu.HBM)
        return pl.pallas_call(
            functools.partial(compute, sizes),
            out_shape=jax.ShapeDtypeStruct((4, rows, part), f32),
            in_specs=[smem, smem] + [anywhere] * (1 + len(consts)),
            out_specs=pl.BlockSpec(memory_space=pltpu.VMEM),
            scratch_shapes=[
                pltpu.VMEM(((planes + 4) * rows, width), bf),
                pltpu.VMEM((4, planes, width), bf),
                pltpu.VMEM((2, planes, width), bf),
                pltpu.VMEM((2, planes, width), bf),
                pltpu.VMEM((4 * ZB, width), bf),
                pltpu.VMEM(((planes + 2) * rows, width), bf),
                pltpu.VMEM((ZB, width), bf),
                pltpu.VMEM((ZB, width), bf),
                pltpu.VMEM(((planes + 2) * rows, width), f32),
                pltpu.VMEM((ZB * rows, width), f32),
                pltpu.VMEM((ZB * rows, width), f32),
                pltpu.VMEM((5 * knot_pos.shape[0], 8, 128), f32),
                pltpu.VMEM((sizes[0], 4, rows, part), f32),
                pltpu.VMEM((sizes[0], 4, rows, part), f32),
                pltpu.VMEM((rows // 8 * (width // 128), knot_pos.shape[0] + 2, 8, 128), f32),
            ]
            + [pltpu.VMEM(c.shape, c.dtype) for c in consts]
            + [
                dma((planes // ZB,)), dma((len(consts),)),
                dma((2,)), dma((2,)),
                dma((2 * planes // ZB,)), dma((2 * planes // ZB,)),
                dma((4,)), dma((4,)),
                dma((sizes[0] - 1,)), dma((sizes[0] - 1,)),
            ],
            compiler_params=pltpu.CompilerParams(
                vmem_limit_bytes=62 << 20, collective_id=0, has_side_effects=True
            ),
        )(knot_pos, knot_color, volume.reshape(planes * rows, width), *consts)

    in_specs = (P("depth", "tile", None), P(), P())
    return jax.shard_map(
        body, mesh=mesh, in_specs=in_specs, out_specs=P(None, "tile", "depth"), check_vma=False
    )
```
